128 devices in a mesh: span: 8 (over z, core), seq: 16 (over x, y).
Axes of the slice: x: 4, y: 4, z: 4, core: 2. Of those that a mesh axis runs over, the one named last changes fastest.
Arguments:
- queries: bfloat16 [8, 2048, 6144], P('span', 'seq'), as said below
- key_states: bfloat16 [8, 2048, 1024], P('span', 'seq'), as said below
- value_states: bfloat16 [8, 2048, 1024], P('span', 'seq'), may hold values from -6 to 6
- block_lists: int32 [8, 8, 8, 8], P('span'), may hold values from -1 to 111, as said below
Outputs:
- attended: bfloat16 [8, 2048, 6144], P('span', 'seq')
The draws below stay inside these ranges and needn't reach their ends.
Inputs may be any that keep to these rules, and one draw needn't show every extreme that they name: `queries`: real numbers. `key_states`: real numbers. `block_lists`: entry [c, g, t, j] is -1 for an unused slot or the number of a block among the first c * 16 blocks, that is, of an earlier span. The used slots of a tile come first, and every tile of a span after the first uses at least one; the first span uses none. In every span after the first some tile uses all 8 slots. Blocks may repeat.
All inputs are finite; a program needn't handle non-finite values.
Results may differ from the reference program's by a relative error of at most 0.0049.
Values may be sent and summed in bfloat16 or wider, within the bound.
No kernel may reach another device: no remote copies, remote signals or barrier semaphores. Data moves between devices by JAX's collectives and lax.ppermute only.
A program may use at most 128 MiB of HBM per device.

```python
import jax
import jax.numpy as jnp
from jax import lax

H = 48
KVH = 8
DH = 128
D = 6144
QT = 256
BK = 128
NSEL = 8
SPANS = 8
SEQ_LEN = 2048
TILES = 8
NB = 16


def shared_normals(key):
    first_key, second_key = jax.random.split(key)
    first_draw = jnp.clip(jax.random.normal(first_key, (SPANS, SEQ_LEN, D), jnp.float32), -6.0, 6.0)
    second_draw = jnp.clip(jax.random.normal(second_key, (SPANS, SEQ_LEN, KVH * DH), jnp.float32), -6.0, 6.0)
    return (first_draw, second_draw)


def draw_queries(key, part):
    base_query, base_key = shared_normals(key)
    return (2.5 * base_query).astype(jnp.bfloat16)


def draw_key_states(key, part):
    base_query, base_key = shared_normals(key)
    return base_key.astype(jnp.bfloat16)


def draw_block_lists(key, part):
    key = jax.random.fold_in(key, 7)
    first_key, second_key = jax.random.split(key)
    shape = (SPANS, KVH, TILES, NSEL)
    span_ids = lax.broadcasted_iota(jnp.int32, shape, 0)
    head_ids = lax.broadcasted_iota(jnp.int32, shape, 1)
    tile_ids = lax.broadcasted_iota(jnp.int32, shape, 2)
    slot_ids = lax.broadcasted_iota(jnp.int32, shape, 3)
    available = span_ids * NB
    raw_ids = jax.random.randint(first_key, shape, 0, 2 ** 30, jnp.int32)
    entries = raw_ids % jnp.maximum(available, 1)
    used_slots = jax.random.randint(second_key, (SPANS, KVH, TILES, 1), 1, NSEL + 1, jnp.int32)
    first_tile = (head_ids[..., :1] == 0) & (tile_ids[..., :1] == 0)
    used_slots = jnp.where(first_tile, NSEL, used_slots)
    live = (slot_ids < used_slots) & (span_ids > 0)
    corner = (span_ids == SPANS - 1) & (head_ids == 0) & (tile_ids == 0) & (slot_ids == 0)
    entries = jnp.where(corner, available - 1, entries)
    return jnp.where(live, entries, -1).astype(jnp.int32)


def shard_levels(own_key, extent, cuts, least, largest):
    gain = 1.0
    for dim, shards_of in cuts:
        draws = jax.random.uniform(jax.random.fold_in(jax.random.fold_in(own_key, 6), dim), (shards_of,), jnp.float32, least / len(cuts), largest / len(cuts))
        gain = gain * jnp.repeat(jnp.exp(draws), extent[dim] // shards_of).reshape((-1,) + (1,) * (len(extent) - 1 - dim))
    return gain


def bell_draw(key, dims, scale, reach, pieces=(), held_as=jnp.bfloat16):
    gain = shard_levels(key, dims, pieces, -0.22, 0.18) if pieces else 1.0
    values = jax.random.normal(key, dims, jnp.float32) * scale * gain
    return jnp.minimum(jnp.maximum(values, -reach), reach).astype(held_as)


def setup_inputs(seed: int = 0) -> dict:
    seeds = jax.random.split(jax.random.key(seed), 5)
    return {
        "queries": draw_queries(jax.random.fold_in(seeds[4], 71), 0),
        "key_states": draw_key_states(jax.random.fold_in(seeds[4], 71), 0),
        "value_states": bell_draw(seeds[2], (SPANS, SEQ_LEN, KVH * DH), 1.0, 6.0, ((0, 8), (1, 16))),
        "block_lists": draw_block_lists(jax.random.fold_in(seeds[4], 71), 0),
    }


def joint_attention(query_rows, own_keys, own_values, far_keys, far_values, usable):
    seq_len = query_rows.shape[0]
    tile_count = seq_len // QT
    scaling = DH ** -0.5
    query_full = query_rows.astype(jnp.float32)
    own_scores = jnp.einsum("qd,kd->qk", query_full, own_keys.astype(jnp.float32), precision=lax.Precision.HIGHEST) * scaling
    own_scores = own_scores.reshape(tile_count, QT, seq_len)
    query_tiles = query_full.reshape(tile_count, QT, DH)
    far_scores = jnp.einsum("tqd,tkd->tqk", query_tiles, far_keys.astype(jnp.float32), precision=lax.Precision.HIGHEST) * scaling
    far_scores = jnp.where(usable[:, None, :], far_scores, -jnp.inf)
    row_max = jnp.maximum(jnp.max(own_scores, axis=-1), jnp.max(far_scores, axis=-1))
    own_exp = jnp.exp(own_scores - row_max[..., None])
    far_exp = jnp.exp(far_scores - row_max[..., None])
    denominator = jnp.sum(own_exp, axis=-1) + jnp.sum(far_exp, axis=-1)
    own_prob = (own_exp / denominator[..., None]).astype(jnp.bfloat16)
    far_prob = (far_exp / denominator[..., None]).astype(jnp.bfloat16)
    result = jnp.einsum("tqk,kd->tqd", own_prob.astype(jnp.float32), own_values.astype(jnp.float32), precision=lax.Precision.HIGHEST)
    result = result + jnp.einsum("tqk,tkd->tqd", far_prob.astype(jnp.float32), far_values.astype(jnp.float32), precision=lax.Precision.HIGHEST)
    return result.reshape(seq_len, DH).astype(jnp.bfloat16)


def reference(queries, key_states, value_states, block_lists):
    group_size = H // KVH
    flat_keys = key_states.reshape(SPANS * SEQ_LEN, KVH, DH)
    flat_values = value_states.reshape(SPANS * SEQ_LEN, KVH, DH)
    results = []
    for span_idx in range(SPANS):
        span_q = queries[span_idx].reshape(SEQ_LEN, H, DH)
        span_k = key_states[span_idx].reshape(SEQ_LEN, KVH, DH)
        span_v = value_states[span_idx].reshape(SEQ_LEN, KVH, DH)
        span_lists = block_lists[span_idx]

        def one_head(head):
            group = (head // group_size).astype(jnp.int32)
            query_rows = lax.dynamic_index_in_dim(span_q, head, 1, keepdims=False)
            own_keys = lax.dynamic_index_in_dim(span_k, group, 1, keepdims=False)
            own_values = lax.dynamic_index_in_dim(span_v, group, 1, keepdims=False)
            every_key = lax.dynamic_index_in_dim(flat_keys, group, 1, keepdims=False).reshape(SPANS * NB, BK, DH)
            every_value = lax.dynamic_index_in_dim(flat_values, group, 1, keepdims=False).reshape(SPANS * NB, BK, DH)
            block_ids = lax.dynamic_index_in_dim(span_lists, group, 0, keepdims=False)
            clipped = jnp.maximum(block_ids, 0).astype(jnp.int32)
            far_keys = every_key[clipped].reshape(TILES, NSEL * BK, DH)
            far_values = every_value[clipped].reshape(TILES, NSEL * BK, DH)
            usable = jnp.repeat(block_ids >= 0, BK, axis=1)
            return joint_attention(query_rows, own_keys, own_values, far_keys, far_values, usable)

        per_head = lax.map(one_head, jnp.arange(H, dtype=jnp.int32))
        results.append(jnp.transpose(per_head, (1, 0, 2)).reshape(SEQ_LEN, D))
    return jnp.stack(results)
```

```python
import functools

import jax
import jax.numpy as jnp
from jax import lax
from jax.experimental import pallas as pl
from jax.experimental.pallas import tpu as pltpu
from jax.sharding import PartitionSpec as P

DH = 128
QT = 256
BK = 128
LOG2E = 1.4426950408889634
VMEM_BYTES = 52 * 2**20


def scaled_query(query_rows):
    scaled = query_rows.astype(jnp.float32) * (LOG2E * DH**-0.5)
    high = scaled.astype(jnp.bfloat16)
    low = (scaled - high.astype(jnp.float32)).astype(jnp.bfloat16)
    return jnp.concatenate([high, low], axis=1)


def scores_of(query_pair, keys_twice):
    return lax.dot_general(
        query_pair, keys_twice, (((1,), (1,)), ((), ())), preferred_element_type=jnp.float32
    )


def own_kernel(heads, q_ref, kv_ref, acc_ref, stat_ref, keys, values):
    rows = kv_ref.shape[0]
    block = kv_ref[:, :DH]
    keys[:, :DH] = block
    keys[:, DH:] = block
    values[:, :DH] = kv_ref[:, DH:]
    values[:, DH:] = jnp.ones((rows, DH), jnp.bfloat16)

    def tile(t, carry):
        at = pl.ds(pl.multiple_of(t * QT, QT), QT)
        for head in range(heads):
            columns = slice(head * DH, (head + 1) * DH)
            scores = scores_of(scaled_query(q_ref[at, columns]), keys[...])
            top = jnp.max(scores, axis=1, keepdims=True)
            weights = jnp.exp2(scores - top).astype(jnp.bfloat16)
            sums = jnp.dot(weights, values[...], preferred_element_type=jnp.float32)
            acc_ref[at, columns] = sums[:, :DH]
            stat_ref[at, head : head + 1] = top
            stat_ref[at, heads + head : heads + head + 1] = sums[:, DH : DH + 1]
        return carry

    lax.fori_loop(0, q_ref.shape[0] // QT, tile, 0)


def far_kernel(heads, tiles, slots, ids_ref, place_ref, q_ref, acc_ref, stat_ref, kv_ref, *rest):
    pieces, (out_ref, keys, values, key_sem, value_sem) = rest[:-5], rest[-5:]
    piece_blocks = pieces[0].shape[0] // BK
    plane, core = place_ref[0], place_ref[1]

    def fetch(source, first, t, j):
        rows = pl.ds(pl.multiple_of(first * BK, BK), BK)
        to = pl.ds(j * BK, BK)
        from_keys = source.at[rows, pl.ds(0, DH)]
        pltpu.make_async_copy(from_keys, keys.at[t, to, pl.ds(0, DH)], key_sem.at[t]).start()
        pltpu.make_async_copy(from_keys, keys.at[t, to, pl.ds(DH, DH)], key_sem.at[t]).start()
        pltpu.make_async_copy(
            source.at[rows, pl.ds(DH, DH)], values.at[t, to, pl.ds(0, DH)], value_sem.at[t]
        ).start()

    for t in range(tiles):
        for j in range(slots):
            block = ids_ref[t * slots + j]
            used = block >= 0
            number = jnp.maximum(block, 0)
            span, within = number // (2 * piece_blocks), number % (2 * piece_blocks)
            back = plane - span // 2
            direct = (span % 2 == core).astype(jnp.int32)
            at = jnp.where(back == 0, 0, 2 + (back - 1) * 4 + direct * 2) + within // piece_blocks
            at = jnp.where(used, at, -1)
            first = within % piece_blocks

            @pl.when(at < 0)
            def _():
                fetch(kv_ref, 0, t, j)

            for n, piece in enumerate(pieces):

                @pl.when(at == n)
                def _():
                    fetch(piece, first, t, j)

    for t in range(tiles):
        pltpu.make_async_copy(keys.at[t], keys.at[t], key_sem.at[t]).wait()
        pltpu.make_async_copy(
            values.at[t, :, pl.ds(0, DH)], values.at[t, :, pl.ds(0, DH)], value_sem.at[t]
        ).wait()
        values[t, :, DH:] = jnp.ones((slots * BK, DH), jnp.bfloat16)
        for j in range(slots):

            @pl.when(ids_ref[t * slots + j] < 0)
            def _():
                values[t, j * BK : (j + 1) * BK, :] = jnp.zeros((BK, 2 * DH), jnp.bfloat16)

        at = slice(t * QT, (t + 1) * QT)
        for head in range(heads):
            columns = slice(head * DH, (head + 1) * DH)
            scores = scores_of(scaled_query(q_ref[at, columns]), keys[t])
            own_top = stat_ref[at, head : head + 1]
            own_total = stat_ref[at, heads + head : heads + head + 1]
            top = jnp.maximum(jnp.max(scores, axis=1, keepdims=True), own_top)
            weights = jnp.exp2(scores - top).astype(jnp.bfloat16)
            sums = jnp.dot(weights, values[t], preferred_element_type=jnp.float32)
            shrink = jnp.exp2(own_top - top)
            total = own_total * shrink + sums[:, DH : DH + 1]
            result = (acc_ref[at, columns] * shrink + sums[:, :DH]) / total
            out_ref[at, columns] = result.astype(jnp.bfloat16)


def own_attention(q, kv):
    tokens, width = q.shape
    heads = width // DH
    whole = pl.BlockSpec(memory_space=pltpu.VMEM)
    scores = tokens * heads * kv.shape[0]
    return pl.pallas_call(
        functools.partial(own_kernel, heads),
        out_shape=(
            jax.ShapeDtypeStruct((tokens, width), jnp.float32),
            jax.ShapeDtypeStruct((tokens, 2 * heads), jnp.float32),
        ),
        in_specs=[whole] * 2,
        out_specs=(whole, whole),
        scratch_shapes=[
            pltpu.VMEM((kv.shape[0], 2 * DH), jnp.bfloat16),
            pltpu.VMEM((kv.shape[0], 2 * DH), jnp.bfloat16),
        ],
        cost_estimate=pl.CostEstimate(
            flops=8 * scores * DH, bytes_accessed=8 * tokens * width, transcendentals=scores
        ),
        compiler_params=pltpu.CompilerParams(vmem_limit_bytes=VMEM_BYTES),
        name="own_attention",
    )(q, kv)


def far_attention(ids, place, q, acc, stats, kv, pieces, tiles, slots):
    tokens, width = q.shape
    heads = width // DH
    whole = pl.BlockSpec(memory_space=pltpu.VMEM)
    scalars = pl.BlockSpec(memory_space=pltpu.SMEM)
    anywhere = pl.BlockSpec(memory_space=pl.ANY)
    scores = tokens * heads * slots * BK
    return pl.pallas_call(
        functools.partial(far_kernel, heads, tiles, slots),
        out_shape=jax.ShapeDtypeStruct((tokens, width), jnp.bfloat16),
        in_specs=[scalars] * 2 + [whole] * 3 + [anywhere] * (1 + len(pieces)),
        out_specs=whole,
        scratch_shapes=[
            pltpu.VMEM((tiles, slots * BK, 2 * DH), jnp.bfloat16),
            pltpu.VMEM((tiles, slots * BK, 2 * DH), jnp.bfloat16),
            pltpu.SemaphoreType.DMA((tiles,)),
            pltpu.SemaphoreType.DMA((tiles,)),
        ],
        cost_estimate=pl.CostEstimate(
            flops=8 * scores * DH, bytes_accessed=8 * tokens * width, transcendentals=scores
        ),
        compiler_params=pltpu.CompilerParams(vmem_limit_bytes=VMEM_BYTES),
        name="far_attention",
    )(ids, place, q, acc, stats, kv, *pieces)


def on_device(queries, key_states, value_states, block_lists):
    tok_rows = queries.shape[1]
    model_width = queries.shape[2]
    kv_heads = key_states.shape[2] // DH
    seq_size, spans = lax.axis_size("seq"), lax.axis_size("span")
    copies = seq_size // kv_heads
    width = model_width // kv_heads
    place = lax.axis_index("seq")
    group, part = place % kv_heads, place // kv_heads
    span = lax.axis_index("span")
    tile_count, slots = block_lists.shape[2], block_lists.shape[3]
    tiles = tile_count // copies
    rings = [list(range(c * kv_heads, (c + 1) * kv_heads)) for c in range(copies)]

    keys = key_states[0].reshape(tok_rows, kv_heads, DH)
    values = value_states[0].reshape(tok_rows, kv_heads, DH)
    kv_send = jnp.transpose(jnp.concatenate([keys, values], axis=2), (1, 0, 2))
    kv_send = jnp.concatenate([kv_send] * copies, axis=0)
    kv = lax.all_to_all(kv_send, "seq", 0, 0, tiled=True).reshape(seq_size * tok_rows, 2 * DH)

    q_send = jnp.transpose(queries[0].reshape(tok_rows, kv_heads, width), (1, 0, 2))
    q = lax.all_to_all(q_send, "seq", 0, 0, tiled=True, axis_index_groups=rings)
    q = q.reshape(kv_heads * tok_rows, width)

    def shift(x, by):
        return lax.ppermute(x, "span", [(i, (i + by) % spans) for i in range(spans)])

    def swap(x):
        return lax.ppermute(x, "span", [(i, i ^ 1) for i in range(spans)])

    half = kv.shape[0] // 2
    first, second = kv[:half], kv[half:]
    up_first = shift(first, 2)
    down_second = shift(second, -2)
    up_second = shift(second, 2)
    down_first = shift(first, -2)
    two_first = shift(up_first, 2)
    two_second = shift(down_second, -2)
    received = [up_first, up_second, two_first, two_second, down_first, down_second]
    pieces = [swap(first), swap(second)]
    for n in range(0, 6, 2):
        pieces += [swap(received[n]), swap(received[n + 1]), received[n], received[n + 1]]

    acc, stats = own_attention(q, kv)
    ids = lax.dynamic_slice(block_lists, (0, group, part * tiles, 0), (1, 1, tiles, slots))
    where = jnp.stack([span // 2, span % 2]).astype(jnp.int32)
    out = far_attention(ids.reshape(tiles * slots), where, q, acc, stats, kv, pieces, tiles, slots)

    out = out.reshape(kv_heads, tok_rows, width)
    back = lax.all_to_all(out, "seq", 0, 0, tiled=True, axis_index_groups=rings)
    return jnp.transpose(back, (1, 0, 2)).reshape(1, tok_rows, model_width)


def solution(mesh):
    in_specs = (
        P("span", "seq", None),
        P("span", "seq", None),
        P("span", "seq", None),
        P("span", None, None, None),
    )
    out_specs = P("span", "seq", None)
    return jax.shard_map(
        on_device, mesh=mesh, in_specs=in_specs, out_specs=out_specs, check_vma=False
    )
```

```python
import functools

import jax
import jax.numpy as jnp
from jax import lax
from jax.experimental import pallas as pl
from jax.experimental.pallas import tpu as pltpu
from jax.sharding import PartitionSpec as P

DH = 128
QT = 256
BK = 128
LOG2E = 1.4426950408889634
VMEM_BYTES = 52 * 2**20


def scaled_query(query_rows):
    scaled = query_rows.astype(jnp.float32) * (LOG2E * DH**-0.5)
    high = scaled.astype(jnp.bfloat16)
    low = (scaled - high.astype(jnp.float32)).astype(jnp.bfloat16)
    return jnp.concatenate([high, low], axis=1)


def scores_of(query_pair, keys_twice):
    return lax.dot_general(
        query_pair, keys_twice, (((1,), (1,)), ((), ())), preferred_element_type=jnp.float32
    )


def own_kernel(heads, q_ref, near_ref, other_ref, acc_ref, stat_ref, keys, values):
    blocks = near_ref.shape[0]
    for n in range(2 * blocks):
        source = near_ref if n < blocks else other_ref
        rows = slice(n * BK, (n + 1) * BK)
        block = source[n % blocks, 0]
        keys[rows, :DH] = block
        keys[rows, DH:] = block
        values[rows, :DH] = source[n % blocks, 1]
    values[:, DH:] = jnp.ones((2 * blocks * BK, DH), jnp.bfloat16)

    def tile(t, carry):
        at = pl.ds(pl.multiple_of(t * QT, QT), QT)
        for head in range(heads):
            columns = slice(head * DH, (head + 1) * DH)
            scores = scores_of(scaled_query(q_ref[at, columns]), keys[...])
            top = jnp.max(scores, axis=1, keepdims=True)
            weights = jnp.exp2(scores - top).astype(jnp.bfloat16)
            sums = jnp.dot(weights, values[...], preferred_element_type=jnp.float32)
            acc_ref[at, columns] = sums[:, :DH]
            stat_ref[at, head : head + 1] = top
            stat_ref[at, heads + head : heads + head + 1] = sums[:, DH : DH + 1]
        return carry

    lax.fori_loop(0, q_ref.shape[0] // QT, tile, 0)


def far_kernel(heads, tiles, slots, chunks, ids_ref, place_ref, q_ref, *rest):
    own = [(rest[2 * n], rest[2 * n + 1]) for n in range(chunks)]
    pieces, (out_ref, keys, values, key_sem, value_sem) = rest[2 * chunks : -5], rest[-5:]
    piece_blocks = pieces[0].shape[0]
    plane, core, part = place_ref[0], place_ref[1], place_ref[2]

    def fetch(source, block, t, j):
        to = pl.ds(pl.multiple_of(j * BK, BK), BK)
        for column in (0, DH):
            pltpu.make_async_copy(
                source.at[block, 0], keys.at[t, to, pl.ds(column, DH)], key_sem.at[t]
            ).start()
        pltpu.make_async_copy(
            source.at[block, 1], values.at[t, to, pl.ds(0, DH)], value_sem.at[t]
        ).start()

    def fetch_from(low, high, at, block, t, j):
        if high - low == 1:
            fetch(pieces[low], block, t, j)
            return
        middle = (low + high) // 2
        lax.cond(
            at < middle,
            lambda: fetch_from(low, middle, at, block, t, j),
            lambda: fetch_from(middle, high, at, block, t, j),
        )

    def slot(n, carry):
        t, j = n // slots, n % slots
        used = ids_ref[n] >= 0
        number = jnp.maximum(ids_ref[n], 0)
        span, within = number // (2 * piece_blocks), number % (2 * piece_blocks)
        half, block = within // piece_blocks, within % piece_blocks
        back = plane - span // 2
        sibling = (span % 2 != core).astype(jnp.int32)
        other = (half != part).astype(jnp.int32)
        at = jnp.where(used, back * 4 + sibling * 2 + other, 0)
        block = jnp.where(used, (block + half * (piece_blocks // 2)) % piece_blocks, 0)
        fetch_from(0, len(pieces), at, block, t, j)
        return carry

    lax.fori_loop(0, tiles * slots, slot, 0)

    for t in range(tiles):
        acc_ref, stat_ref = own[t * chunks // tiles]
        pltpu.make_async_copy(keys.at[t], keys.at[t], key_sem.at[t]).wait()
        pltpu.make_async_copy(
            values.at[t, :, pl.ds(0, DH)], values.at[t, :, pl.ds(0, DH)], value_sem.at[t]
        ).wait()
        values[t, :, DH:] = jnp.ones((slots * BK, DH), jnp.bfloat16)
        for j in range(slots):

            @pl.when(ids_ref[t * slots + j] < 0)
            def _():
                values[t, j * BK : (j + 1) * BK, :] = jnp.zeros((BK, 2 * DH), jnp.bfloat16)

        at = slice(t * QT, (t + 1) * QT)
        first = (t % (tiles // chunks)) * QT
        own_at = slice(first, first + QT)
        for head in range(heads):
            columns = slice(head * DH, (head + 1) * DH)
            scores = scores_of(scaled_query(q_ref[at, columns]), keys[t])
            own_top = stat_ref[own_at, head : head + 1]
            own_total = stat_ref[own_at, heads + head : heads + head + 1]
            top = jnp.maximum(jnp.max(scores, axis=1, keepdims=True), own_top)
            weights = jnp.exp2(scores - top).astype(jnp.bfloat16)
            sums = jnp.dot(weights, values[t], preferred_element_type=jnp.float32)
            shrink = jnp.exp2(own_top - top)
            total = own_total * shrink + sums[:, DH : DH + 1]
            result = (acc_ref[own_at, columns] * shrink + sums[:, :DH]) / total
            out_ref[at, columns] = result.astype(jnp.bfloat16)


def own_attention(q, near, other, chunk, chunks):
    tokens, width = q.shape[0] // chunks, q.shape[1]
    heads = width // DH
    keys = 2 * near.shape[0] * BK
    whole = pl.BlockSpec(memory_space=pltpu.VMEM)
    scores = tokens * heads * keys
    return pl.pallas_call(
        functools.partial(own_kernel, heads),
        grid=(1,),
        out_shape=(
            jax.ShapeDtypeStruct((tokens, width), jnp.float32),
            jax.ShapeDtypeStruct((tokens, 2 * heads), jnp.float32),
        ),
        in_specs=[pl.BlockSpec((tokens, width), lambda _: (chunk, 0)), whole, whole],
        out_specs=(whole, whole),
        scratch_shapes=[pltpu.VMEM((keys, 2 * DH), jnp.bfloat16)] * 2,
        cost_estimate=pl.CostEstimate(
            flops=8 * scores * DH, bytes_accessed=8 * tokens * width, transcendentals=scores
        ),
        compiler_params=pltpu.CompilerParams(vmem_limit_bytes=VMEM_BYTES),
        name="own_attention",
    )(q, near, other)


def far_attention(ids, place, q, own, pieces, tiles, slots):
    tokens, width = q.shape
    heads = width // DH
    whole = pl.BlockSpec(memory_space=pltpu.VMEM)
    scalars = pl.BlockSpec(memory_space=pltpu.SMEM)
    anywhere = pl.BlockSpec(memory_space=pl.ANY)
    scores = tokens * heads * slots * BK
    return pl.pallas_call(
        functools.partial(far_kernel, heads, tiles, slots, len(own)),
        out_shape=jax.ShapeDtypeStruct((tokens, width), jnp.bfloat16),
        in_specs=[scalars] * 2 + [whole] * (1 + 2 * len(own)) + [anywhere] * len(pieces),
        out_specs=whole,
        scratch_shapes=[
            pltpu.VMEM((tiles, slots * BK, 2 * DH), jnp.bfloat16),
            pltpu.VMEM((tiles, slots * BK, 2 * DH), jnp.bfloat16),
            pltpu.SemaphoreType.DMA((tiles,)),
            pltpu.SemaphoreType.DMA((tiles,)),
        ],
        cost_estimate=pl.CostEstimate(
            flops=8 * scores * DH, bytes_accessed=8 * tokens * width, transcendentals=scores
        ),
        compiler_params=pltpu.CompilerParams(vmem_limit_bytes=VMEM_BYTES),
        name="far_attention",
    )(ids, place, q, *[x for pair in own for x in pair], *pieces)


def on_device(queries, key_states, value_states, block_lists):
    tok_rows = queries.shape[1]
    model_width = queries.shape[2]
    kv_heads = key_states.shape[2] // DH
    seq_size, spans = lax.axis_size("seq"), lax.axis_size("span")
    width = model_width // kv_heads
    place = lax.axis_index("seq")
    part = place // kv_heads
    turned = kv_heads // 2
    group = (place + part * turned) % kv_heads
    span = lax.axis_index("span")
    tile_count, slots = block_lists.shape[2], block_lists.shape[3]
    tiles = tile_count // 2
    rings = [
        [c * kv_heads + (j + c * turned) % kv_heads for j in range(kv_heads)] for c in range(2)
    ]

    def turn(x):
        return lax.ppermute(x, "seq", [pair for a, b in zip(*rings) for pair in ((a, b), (b, a))])

    def shift(x, by):
        return lax.ppermute(x, "span", [(i, (i + by) % spans) for i in range(spans)])

    def swap(x):
        return lax.ppermute(x, "span", [(i, i ^ 1) for i in range(spans)])

    def by_head(x, columns):
        return jnp.transpose(x[0].reshape(tok_rows, kv_heads, columns), (1, 0, 2))

    kv_send = jnp.stack([by_head(key_states, DH), by_head(value_states, DH)], axis=1)
    near = lax.all_to_all(kv_send, "seq", 0, 0, tiled=True, axis_index_groups=rings)
    other = turn(near)
    q_send = by_head(queries, width)
    q = lax.all_to_all(q_send, "seq", 0, 0, tiled=True, axis_index_groups=rings)
    q = q.reshape(kv_heads * tok_rows, width)

    up_near = shift(near, 2)
    down_near = shift(near, -2)
    up_other = shift(other, 2)
    down_other = shift(other, -2)
    two_near = shift(up_near, 2)
    own_swaps = [swap(near), swap(other)]
    own = [own_attention(q, near, other, 0, 2)]
    (own[0], down_other, two_near) = lax.optimization_barrier((own[0], down_other, two_near))
    two_other = shift(down_other, -2)
    own.append(own_attention(q, near, other, 1, 2))
    late = (two_near, two_other, up_near, up_other, down_near, down_other)
    late, own[1] = lax.optimization_barrier((late, own[1]))
    two_near, two_other, up_near, up_other, down_near, down_other = late
    pieces = [near, other] + own_swaps
    for pair in ((up_near, up_other), (two_near, two_other), (down_near, down_other)):
        pieces += list(pair) + [swap(x) for x in pair]
    ids = lax.dynamic_slice(block_lists, (0, group, part * tiles, 0), (1, 1, tiles, slots))[0, 0]
    ids = jnp.where(part == 0, ids, jnp.roll(ids, tiles // 2, axis=0))
    where = jnp.stack([span // 2, span % 2, part]).astype(jnp.int32)
    out = far_attention(ids.reshape(tiles * slots), where, q, own, pieces, tiles, slots)

    out = out.reshape(kv_heads, tok_rows, width)
    back = lax.all_to_all(out, "seq", 0, 0, tiled=True, axis_index_groups=rings)
    return jnp.transpose(back, (1, 0, 2)).reshape(1, tok_rows, model_width)


def solution(mesh):
    in_specs = (
        P("span", "seq", None),
        P("span", "seq", None),
        P("span", "seq", None),
        P("span", None, None, None),
    )
    out_specs = P("span", "seq", None)
    return jax.shard_map(
        on_device, mesh=mesh, in_specs=in_specs, out_specs=out_specs, check_vma=False
    )
```

```python
import functools

import jax
import jax.numpy as jnp
from jax import lax
from jax.experimental import pallas as pl
from jax.experimental.pallas import tpu as pltpu
from jax.sharding import PartitionSpec as P

DH = 128
QT = 256
BK = 128
LOG2E = 1.4426950408889634
VMEM_BYTES = 52 * 2**20


def scaled_query(query_rows):
    scaled = query_rows.astype(jnp.float32) * (LOG2E * DH**-0.5)
    high = scaled.astype(jnp.bfloat16)
    low = (scaled - high.astype(jnp.float32)).astype(jnp.bfloat16)
    return jnp.concatenate([high, low], axis=1)


def scores_of(query_pair, keys_twice):
    return lax.dot_general(
        query_pair, keys_twice, (((1,), (1,)), ((), ())), preferred_element_type=jnp.float32
    )


def pack_kernel(k_ref, v_ref, out_ref):
    for head in range(out_ref.shape[0]):
        columns = slice(head * DH, (head + 1) * DH)
        out_ref[head, :, :DH] = k_ref[0, :, columns]
        out_ref[head, :, DH:] = v_ref[0, :, columns]


def own_kernel(heads, q_ref, near_ref, other_ref, acc_ref, stat_ref, keys, values):
    blocks = near_ref.shape[0]
    for n in range(2 * blocks):
        source = near_ref if n < blocks else other_ref
        rows = slice(n * BK, (n + 1) * BK)
        block = source[n % blocks, :, :DH]
        keys[rows, :DH] = block
        keys[rows, DH:] = block
        values[rows, :DH] = source[n % blocks, :, DH:]
    values[:, DH:] = jnp.ones((2 * blocks * BK, DH), jnp.bfloat16)

    def tile(t, carry):
        at = pl.ds(pl.multiple_of(t * QT, QT), QT)
        for head in range(heads):
            columns = slice(head * DH, (head + 1) * DH)
            scores = scores_of(scaled_query(q_ref[at, columns]), keys[...])
            top = jnp.max(scores, axis=1, keepdims=True)
            weights = jnp.exp2(scores - top).astype(jnp.bfloat16)
            sums = jnp.dot(weights, values[...], preferred_element_type=jnp.float32)
            total = sums[:, DH:]
            acc_ref[at, columns] = sums[:, :DH] / total
            stat_ref[at, head : head + 1] = (top + jnp.log2(total))[:, :1]
        return carry

    lax.fori_loop(0, q_ref.shape[0] // QT, tile, 0)


def far_kernel(heads, tiles, slots, chunks, ids_ref, place_ref, q_ref, *rest):
    own = [(rest[2 * n], rest[2 * n + 1]) for n in range(chunks)]
    pieces, (out_ref, far, ready) = rest[2 * chunks : -3], rest[-3:]
    piece_blocks = pieces[0].shape[0]
    bits = piece_blocks.bit_length() - 1
    plane, core, part = place_ref[0], place_ref[1], place_ref[2]

    def fetch(source, block, t, j):
        to = pl.ds(pl.multiple_of(j * BK, BK), BK)
        pltpu.make_async_copy(
            source.at[block], far.at[t, to, pl.ds(DH, 2 * DH)], ready.at[t]
        ).start()

    def fetch_from(low, high, at, block, t, j):
        if high - low == 1:
            fetch(pieces[low], block, t, j)
            return
        middle = (low + high) // 2
        lax.cond(
            at < middle,
            lambda: fetch_from(low, middle, at, block, t, j),
            lambda: fetch_from(middle, high, at, block, t, j),
        )

    for t in range(tiles):

        def slot(j, carry):
            listed = ids_ref[t * slots + j]
            number = jnp.maximum(listed, 0)
            span, half = number >> (bits + 1), (number >> bits) & 1
            back = plane - (span >> 1)
            at = back * 4 + ((span & 1) ^ core) * 2 + (half ^ part)
            at = jnp.where(listed >= 0, at, 0)
            block = (number & (piece_blocks - 1)) ^ (half * (piece_blocks // 2))
            block = jnp.where(listed >= 0, block, 0)
            fetch_from(0, len(pieces), at, block, t, j)
            return carry

        lax.fori_loop(0, slots, slot, 0)

    for t in range(tiles):
        acc_ref, stat_ref = own[t * chunks // tiles]
        landed = far.at[t, :, pl.ds(DH, 2 * DH)]
        pltpu.make_async_copy(landed, landed, ready.at[t]).wait()
        far[t, :, :DH] = far[t, :, DH : 2 * DH]
        far[t, :, 3 * DH :] = jnp.ones((slots * BK, DH), jnp.bfloat16)
        for j in range(slots):

            @pl.when(ids_ref[t * slots + j] < 0)
            def _():
                far[t, j * BK : (j + 1) * BK, 2 * DH :] = jnp.zeros((BK, 2 * DH), jnp.bfloat16)

        at = slice(t * QT, (t + 1) * QT)
        first = (t % (tiles // chunks)) * QT
        own_at = slice(first, first + QT)
        columns = [slice(head * DH, (head + 1) * DH) for head in range(heads)]
        keys, values = far[t, :, : 2 * DH], far[t, :, 2 * DH :]
        scores = [scores_of(scaled_query(q_ref[at, column]), keys) for column in columns]
        own_size = [stat_ref[own_at, head : head + 1] for head in range(heads)]
        tops = [
            jnp.maximum(jnp.max(score, axis=1, keepdims=True), size)
            for score, size in zip(scores, own_size)
        ]
        weights = [jnp.exp2(score - top).astype(jnp.bfloat16) for score, top in zip(scores, tops)]
        sums = [jnp.dot(w, values, preferred_element_type=jnp.float32) for w in weights]
        for head, column in enumerate(columns):
            share = jnp.exp2(own_size[head] - tops[head])
            total = share + sums[head][:, DH:]
            result = (acc_ref[own_at, column] * share + sums[head][:, :DH]) / total
            out_ref[at, column] = result.astype(jnp.bfloat16)


def pack(key_states, value_states):
    rows, heads = key_states.shape[1], key_states.shape[2] // DH
    whole = pl.BlockSpec(memory_space=pltpu.VMEM)
    return pl.pallas_call(
        pack_kernel,
        out_shape=jax.ShapeDtypeStruct((heads, rows, 2 * DH), key_states.dtype),
        in_specs=[whole] * 2,
        out_specs=whole,
        name="pack",
    )(key_states, value_states)


def own_attention(q, near, other, chunk, chunks):
    tokens, width = q.shape[0] // chunks, q.shape[1]
    heads = width // DH
    keys = 2 * near.shape[0] * BK
    whole = pl.BlockSpec(memory_space=pltpu.VMEM)
    scores = tokens * heads * keys
    return pl.pallas_call(
        functools.partial(own_kernel, heads),
        grid=(1,),
        out_shape=(
            jax.ShapeDtypeStruct((tokens, width), jnp.float32),
            jax.ShapeDtypeStruct((tokens, heads), jnp.float32),
        ),
        in_specs=[pl.BlockSpec((tokens, width), lambda _: (chunk, 0)), whole, whole],
        out_specs=(whole, whole),
        scratch_shapes=[pltpu.VMEM((keys, 2 * DH), jnp.bfloat16)] * 2,
        cost_estimate=pl.CostEstimate(
            flops=8 * scores * DH, bytes_accessed=8 * tokens * width, transcendentals=scores
        ),
        compiler_params=pltpu.CompilerParams(vmem_limit_bytes=VMEM_BYTES),
        name="own_attention",
    )(q, near, other)


def far_attention(ids, place, q, own, pieces, tiles, slots):
    tokens, width = q.shape
    heads = width // DH
    whole = pl.BlockSpec(memory_space=pltpu.VMEM)
    scalars = pl.BlockSpec(memory_space=pltpu.SMEM)
    anywhere = pl.BlockSpec(memory_space=pl.ANY)
    scores = tokens * heads * slots * BK
    return pl.pallas_call(
        functools.partial(far_kernel, heads, tiles, slots, len(own)),
        out_shape=jax.ShapeDtypeStruct((tokens, width), jnp.bfloat16),
        in_specs=[scalars] * 2 + [whole] * (1 + 2 * len(own)) + [anywhere] * len(pieces),
        out_specs=whole,
        scratch_shapes=[
            pltpu.VMEM((tiles, slots * BK, 4 * DH), jnp.bfloat16),
            pltpu.SemaphoreType.DMA((tiles,)),
        ],
        cost_estimate=pl.CostEstimate(
            flops=8 * scores * DH, bytes_accessed=8 * tokens * width, transcendentals=scores
        ),
        compiler_params=pltpu.CompilerParams(vmem_limit_bytes=VMEM_BYTES),
        name="far_attention",
    )(ids, place, q, *[x for pair in own for x in pair], *pieces)


def on_device(queries, key_states, value_states, block_lists):
    tok_rows = queries.shape[1]
    model_width = queries.shape[2]
    kv_heads = key_states.shape[2] // DH
    spans = lax.axis_size("span")
    width = model_width // kv_heads
    place = lax.axis_index("seq")
    part = place // kv_heads
    turned = kv_heads // 2
    group = (place % kv_heads) ^ (part * turned)
    span = lax.axis_index("span")
    tile_count, slots = block_lists.shape[2], block_lists.shape[3]
    tiles = tile_count // 2
    rings = [[c * kv_heads + (j ^ (c * turned)) for j in range(kv_heads)] for c in range(2)]

    def turn(x):
        return lax.ppermute(x, "seq", [pair for a, b in zip(*rings) for pair in ((a, b), (b, a))])

    def shift(x, by):
        return lax.ppermute(x, "span", [(i, (i + by) % spans) for i in range(spans)])

    def swap(x):
        return lax.ppermute(x, "span", [(i, i ^ 1) for i in range(spans)])

    sent = pack(key_states, value_states)
    near = lax.all_to_all(sent, "seq", 0, 0, tiled=True, axis_index_groups=rings)
    q_send = jnp.transpose(queries[0].reshape(tok_rows, kv_heads, width), (1, 0, 2))
    q = lax.all_to_all(q_send, "seq", 0, 0, tiled=True, axis_index_groups=rings)
    q = q.reshape(kv_heads * tok_rows, width)

    other = turn(near)

    up_near = shift(near, 2)
    down_near = shift(near, -2)
    up_other = shift(other, 2)
    down_other = shift(other, -2)
    two_near = shift(up_near, 2)
    swap_near, swap_other = swap(near), swap(other)
    early = (q, up_near, down_near, swap_near, swap_other)
    q, up_near, down_near, swap_near, swap_other = lax.optimization_barrier(early)
    swap_up, swap_down = swap(up_near), swap(down_near)
    own = [own_attention(q, near, other, 0, 2)]
    between = (own[0], q, down_other, swap_up, swap_down)
    own[0], q, down_other, swap_up, swap_down = lax.optimization_barrier(between)
    two_other = shift(down_other, -2)
    own.append(own_attention(q, near, other, 1, 2))
    late = (own[1], two_near, two_other, up_other, down_other)
    own[1], two_near, two_other, up_other, down_other = lax.optimization_barrier(late)
    pieces = [near, other, swap_near, swap_other]
    pieces += [up_near, up_other, swap_up, swap(up_other)]
    pieces += [two_near, two_other, swap(two_near), swap(two_other)]
    pieces += [down_near, down_other, swap_down, swap(down_other)]
    ids = lax.dynamic_slice(block_lists, (0, group, part * tiles, 0), (1, 1, tiles, slots))[0, 0]
    ids = jnp.where(part == 0, ids, jnp.roll(ids, tiles // 2, axis=0))
    where = jnp.stack([span // 2, span % 2, part]).astype(jnp.int32)
    out = far_attention(ids.reshape(tiles * slots), where, q, own, pieces, tiles, slots)

    out = out.reshape(kv_heads, tok_rows, width)
    back = lax.all_to_all(out, "seq", 0, 0, tiled=True, axis_index_groups=rings)
    return jnp.transpose(back, (1, 0, 2)).reshape(1, tok_rows, model_width)


def solution(mesh):
    in_specs = (
        P("span", "seq", None),
        P("span", "seq", None),
        P("span", "seq", None),
        P("span", None, None, None),
    )
    out_specs = P("span", "seq", None)
    return jax.shard_map(
        on_device, mesh=mesh, in_specs=in_specs, out_specs=out_specs, check_vma=False
    )
```

```python
import functools

import jax
import jax.numpy as jnp
from jax import lax
from jax.experimental import pallas as pl
from jax.experimental.pallas import tpu as pltpu
from jax.sharding import PartitionSpec as P

DH = 128
QT = 256
BK = 128
LOG2E = 1.4426950408889634
OWN_VMEM = 16 * 2**20
OWN_SLOTS = 64
FAR_VMEM = 16 * 2**20


def scaled_query(query_rows):
    scaled = query_rows.astype(jnp.float32) * (LOG2E * DH**-0.5)
    high = scaled.astype(jnp.bfloat16)
    low = (scaled - high.astype(jnp.float32)).astype(jnp.bfloat16)
    return jnp.concatenate([high, low], axis=1)


def scores_of(query_pair, keys_twice):
    return lax.dot_general(
        query_pair, keys_twice, (((1,), (1,)), ((), ())), preferred_element_type=jnp.float32
    )


def pack_kernel(k_ref, v_ref, out_ref):
    for head in range(out_ref.shape[0]):
        columns = slice(head * DH, (head + 1) * DH)
        out_ref[head, :, :DH] = k_ref[0, :, columns]
        out_ref[head, :, DH:] = v_ref[0, :, columns]


def own_kernel(heads, steps, place_ref, q_ref, kv_ref, *rest):
    own_ref, keys, values, held, sent = rest[-5:]
    wide = heads * DH
    blocks = kv_ref.shape[0]
    for n in range(blocks):
        rows = slice(n * BK, (n + 1) * BK)
        block = kv_ref[n, :, :DH]
        keys[rows, :DH] = block
        keys[rows, DH:] = block
        values[rows, :DH] = kv_ref[n, :, DH:]
    values[:, DH:] = jnp.ones((blocks * BK, DH), jnp.bfloat16)

    def tile(n, step):
        tile_at = pl.ds(pl.multiple_of(((place_ref[3] >> 1) ^ step) * QT, QT), QT)
        for head in range(heads):
            columns = slice(head * DH, (head + 1) * DH)
            scores = scores_of(scaled_query(q_ref[tile_at, columns]), keys[...])
            top = jnp.max(scores, axis=1, keepdims=True)
            weights = jnp.exp2(scores - top).astype(jnp.bfloat16)
            sums = jnp.dot(weights, values[...], preferred_element_type=jnp.float32)
            total = sums[:, DH:]
            held[n, :, columns] = sums[:, :DH] / total
            held[n, :, wide + head : wide + head + 1] = (top + jnp.log2(total))[:, :1]
        pltpu.make_async_copy(held.at[n], own_ref.at[n], sent.at[n]).start()

    for n, step in enumerate(steps):
        tile(n, step)
    for n in range(len(steps)):
        pltpu.make_async_copy(held.at[n], own_ref.at[n], sent.at[n]).wait()


def far_kernel(heads, steps, slots, ids_ref, place_ref, q_ref, *rest):
    outs = len(steps) * 2
    own_ref, rest = rest[0], rest[1:]
    pieces, out_refs, (far, held, ready, here) = rest[: -4 - outs], rest[-4 - outs : -4], rest[-4:]
    wide = heads * DH
    for n, step in enumerate(steps):
        pltpu.make_async_copy(own_ref.at[step], held.at[n], here.at[n]).start()
    half_blocks = pieces[0].shape[0] // 2
    bits = half_blocks.bit_length() - 1
    plane, core, part, place = [place_ref[n] for n in range(4)]
    tiles = [(place >> 1) ^ step for step in steps]

    def fetch(source, block, n, j):
        to = pl.ds(pl.multiple_of(j * BK, BK), BK)
        pltpu.make_async_copy(
            source.at[block], far.at[n, to, pl.ds(DH, 2 * DH)], ready.at[n]
        ).start()

    def fetch_from(low, high, at, block, n, j):
        if high - low == 1:
            fetch(pieces[low], block, n, j)
            return
        middle = (low + high) // 2
        lax.cond(
            at < middle,
            lambda: fetch_from(low, middle, at, block, n, j),
            lambda: fetch_from(middle, high, at, block, n, j),
        )

    for n, tile in enumerate(tiles):

        def slot(j, carry):
            listed = ids_ref[tile * slots + j]
            number = jnp.maximum(listed, 0)
            span, half = number >> (bits + 1), (number >> bits) & 1
            back = plane - (span >> 1)
            sibling, other = (span & 1) ^ core, half ^ part
            block = (number & (half_blocks - 1)) ^ (half * (half_blocks // 2))
            apart = back == 2
            at = back * 2 + sibling + jnp.where(apart, sibling + other, 0) + 2 * (back >> 1) * (back & 1)
            block = jnp.where(apart, block, block + other * half_blocks)
            at, block = jnp.where(listed >= 0, at, 0), jnp.where(listed >= 0, block, 0)
            fetch_from(0, len(pieces), at, block, n, j)
            return carry

        lax.fori_loop(0, slots, slot, 0)

    for n, tile in enumerate(tiles):
        landed = far.at[n, :, pl.ds(DH, 2 * DH)]
        pltpu.make_async_copy(landed, landed, ready.at[n]).wait()
        far[n, :, :DH] = far[n, :, DH : 2 * DH]
        far[n, :, 3 * DH :] = jnp.ones((slots * BK, DH), jnp.bfloat16)
        for j in range(slots):

            @pl.when(ids_ref[tile * slots + j] < 0)
            def _():
                far[n, j * BK : (j + 1) * BK, 2 * DH :] = jnp.zeros((BK, 2 * DH), jnp.bfloat16)

        at = pl.ds(pl.multiple_of(tile * QT, QT), QT)
        pltpu.make_async_copy(own_ref.at[0], held.at[n], here.at[n]).wait()
        columns = [slice(head * DH, (head + 1) * DH) for head in range(heads)]
        keys, values = far[n, :, : 2 * DH], far[n, :, 2 * DH :]
        scores = [scores_of(scaled_query(q_ref[at, column]), keys) for column in columns]
        own_size = [held[n, :, wide + head : wide + head + 1] for head in range(heads)]
        tops = [
            jnp.maximum(jnp.max(score, axis=1, keepdims=True), size)
            for score, size in zip(scores, own_size)
        ]
        weights = [jnp.exp2(score - top).astype(jnp.bfloat16) for score, top in zip(scores, tops)]
        sums = [jnp.dot(w, values, preferred_element_type=jnp.float32) for w in weights]
        for head, column in enumerate(columns):
            share = jnp.exp2(own_size[head] - tops[head])
            total = share + sums[head][:, DH:]
            result = (held[n, :, column] * share + sums[head][:, :DH]) / total
            upper, lower = result[: QT // 2], result[QT // 2 :]
            odd = (place & 1) == 1
            out_refs[2 * n][:, column] = jnp.where(odd, lower, upper).astype(jnp.bfloat16)
            out_refs[2 * n + 1][:, column] = jnp.where(odd, upper, lower).astype(jnp.bfloat16)


def unpack_kernel(place_ref, *refs):
    width = refs[0].shape[1]
    for step, ref in enumerate(refs[:-1]):
        at = pl.multiple_of((place_ref[3] ^ step) * width, width)
        refs[-1][0, :, pl.ds(at, width)] = ref[...]


def pack(key_states, value_states):
    rows, heads = key_states.shape[1], key_states.shape[2] // DH
    whole = pl.BlockSpec(memory_space=pltpu.VMEM)
    return pl.pallas_call(
        pack_kernel,
        out_shape=jax.ShapeDtypeStruct((heads, rows, 2 * DH), key_states.dtype),
        in_specs=[whole] * 2,
        out_specs=whole,
        name="pack",
    )(key_states, value_states)


def unpack(place, parts):
    rows, width = parts[0].shape
    whole = pl.BlockSpec(memory_space=pltpu.VMEM)
    return pl.pallas_call(
        unpack_kernel,
        out_shape=jax.ShapeDtypeStruct((1, rows, width * len(parts)), parts[0].dtype),
        in_specs=[pl.BlockSpec(memory_space=pltpu.SMEM)] + [whole] * len(parts),
        out_specs=whole,
        name="unpack",
    )(place, *parts)


def own_attention(place, q, kv, steps, after):
    tiles = len(steps)
    tokens, width = tiles * QT, q.shape[1]
    heads = width // DH
    keys = kv.shape[0] * BK
    whole = pl.BlockSpec(memory_space=pltpu.VMEM)
    scores = tokens * heads * keys
    return pl.pallas_call(
        functools.partial(own_kernel, heads, steps),
        out_shape=jax.ShapeDtypeStruct((OWN_SLOTS, QT, width + DH), jnp.float32),
        in_specs=[pl.BlockSpec(memory_space=pltpu.SMEM)]
        + [whole] * 2
        + [pl.BlockSpec(memory_space=pl.ANY)] * len(after),
        out_specs=pl.BlockSpec(memory_space=pl.ANY),
        scratch_shapes=[pltpu.VMEM((keys, 2 * DH), jnp.bfloat16)] * 2
        + [pltpu.VMEM((tiles, QT, width + DH), jnp.float32), pltpu.SemaphoreType.DMA((tiles,))],
        cost_estimate=pl.CostEstimate(
            flops=8 * scores * DH, bytes_accessed=8 * tokens * width, transcendentals=scores
        ),
        compiler_params=pltpu.CompilerParams(vmem_limit_bytes=OWN_VMEM),
        name="own_attention",
    )(place, q, kv, *after)


def far_attention(ids, place, q, own, pieces, steps, slots):
    width = q.shape[1]
    heads = width // DH
    whole = pl.BlockSpec(memory_space=pltpu.VMEM)
    scalars = pl.BlockSpec(memory_space=pltpu.SMEM)
    anywhere = pl.BlockSpec(memory_space=pl.ANY)
    scores = len(steps) * QT * heads * slots * BK
    return pl.pallas_call(
        functools.partial(far_kernel, heads, steps, slots),
        out_shape=[jax.ShapeDtypeStruct((QT // 2, width), jnp.bfloat16)] * (2 * len(steps)),
        in_specs=[scalars] * 2
        + [whole]
        + [anywhere] * (1 + len(pieces)),
        out_specs=[whole] * (2 * len(steps)),
        scratch_shapes=[
            pltpu.VMEM((len(steps), slots * BK, 4 * DH), jnp.bfloat16),
            pltpu.VMEM((len(steps), QT, width + DH), jnp.float32),
            pltpu.SemaphoreType.DMA((len(steps),)),
            pltpu.SemaphoreType.DMA((len(steps),)),
        ],
        cost_estimate=pl.CostEstimate(
            flops=8 * scores * DH, bytes_accessed=8 * q.size, transcendentals=scores
        ),
        compiler_params=pltpu.CompilerParams(vmem_limit_bytes=FAR_VMEM),
        name="far_attention",
    )(ids, place, q, own, *pieces)


def on_device(queries, key_states, value_states, block_lists):
    tok_rows = queries.shape[1]
    model_width = queries.shape[2]
    kv_heads = key_states.shape[2] // DH
    spans = lax.axis_size("span")
    width = model_width // kv_heads
    place = lax.axis_index("seq")
    part = place // kv_heads
    turned = kv_heads // 2
    group = (place % kv_heads) ^ (part * turned)
    span = lax.axis_index("span")
    tile_count, slots = block_lists.shape[2], block_lists.shape[3]
    tiles = tile_count // 2
    rings = [[c * kv_heads + (j ^ (c * turned)) for j in range(kv_heads)] for c in range(2)]

    def turn(x):
        return lax.ppermute(x, "seq", [pair for a, b in zip(*rings) for pair in ((a, b), (b, a))])

    def trade(x, step):
        pairs = [(ring[j], ring[j ^ step]) for ring in rings for j in range(kv_heads)]
        return lax.ppermute(x, "seq", pairs)

    def shift(x, by):
        return lax.ppermute(x, "span", [(i, (i + by) % spans) for i in range(spans)])

    def swap(x):
        return lax.ppermute(x, "span", [(i, i ^ 1) for i in range(spans)])

    where = jnp.stack([span // 2, span % 2, part, group]).astype(jnp.int32)
    sent = pack(key_states, value_states)
    near = lax.all_to_all(sent, "seq", 0, 0, tiled=True, axis_index_groups=rings)
    q_send = jnp.transpose(queries[0].reshape(tok_rows, kv_heads, width), (1, 0, 2))
    q = lax.all_to_all(q_send, "seq", 0, 0, tiled=True, axis_index_groups=rings)
    q = q.reshape(kv_heads * tok_rows, width)

    other = turn(near)
    two_near = shift(near, 4)
    kv = jnp.concatenate([near, other], axis=0)
    up, down = shift(kv, 2), shift(kv, -2)
    two_other = turn(two_near)
    swap_kv, swap_two = swap(kv), swap(two_near)
    own = own_attention(where, q, kv, range(tiles), [])
    own, up, down, two_other = lax.optimization_barrier((own, up, down, two_other))
    pieces = [kv, swap_kv, up, swap(up), two_near, two_other, swap_two, swap(two_other)]
    pieces += [down, swap(down)]
    ids = lax.dynamic_slice(block_lists, (0, group, part * tiles, 0), (1, 1, tiles, slots))[0, 0]
    ids = jnp.where(part == 0, ids, jnp.roll(ids, tiles // 2, axis=0))
    ids = ids.reshape(tiles * slots)
    parts = [None] * kv_heads
    for steps in ((2, 1), (3, 0)):
        results = far_attention(ids, where, q, own, pieces, steps, slots)
        for n, step in enumerate(steps):
            parts[2 * step] = results[2 * n]
            parts[2 * step + 1] = results[2 * n + 1]
        for step in [s for t in steps for s in (2 * t, 2 * t + 1) if s]:
            parts[step] = trade(parts[step], step)
    return unpack(where, parts)


def solution(mesh):
    in_specs = (
        P("span", "seq", None),
        P("span", "seq", None),
        P("span", "seq", None),
        P("span", None, None, None),
    )
    out_specs = P("span", "seq", None)
    return jax.shard_map(
        on_device, mesh=mesh, in_specs=in_specs, out_specs=out_specs, check_vma=False
    )
```

```python
import functools

import jax
import jax.numpy as jnp
from jax import lax
from jax.experimental import pallas as pl
from jax.experimental.pallas import tpu as pltpu
from jax.sharding import PartitionSpec as P

DH = 128
QT = 256
BK = 128
LOG2E = 1.4426950408889634
OWN_VMEM = 16 * 2**20
OWN_SLOTS = 64
FAR_VMEM = 22 * 2**20


def scaled_query(query_rows):
    scaled = query_rows.astype(jnp.float32) * (LOG2E * DH**-0.5)
    high = scaled.astype(jnp.bfloat16)
    low = (scaled - high.astype(jnp.float32)).astype(jnp.bfloat16)
    return jnp.concatenate([high, low], axis=1)


def scores_of(query_pair, keys_twice):
    return lax.dot_general(
        query_pair, keys_twice, (((1,), (1,)), ((), ())), preferred_element_type=jnp.float32
    )


def pack_kernel(k_ref, v_ref, out_ref):
    for head in range(out_ref.shape[0]):
        columns = slice(head * DH, (head + 1) * DH)
        out_ref[head, :, :DH] = k_ref[0, :, columns]
        out_ref[head, :, DH:] = v_ref[0, :, columns]


def own_kernel(heads, steps, place_ref, q_ref, kv_ref, *rest):
    own_ref, keys, values, held, sent = rest[-5:]
    wide = heads * DH
    blocks = kv_ref.shape[0]
    for n in range(blocks):
        rows = slice(n * BK, (n + 1) * BK)
        block = kv_ref[n, :, :DH]
        keys[rows, :DH] = block
        keys[rows, DH:] = block
        values[rows, :DH] = kv_ref[n, :, DH:]
    values[:, DH:] = jnp.ones((blocks * BK, DH), jnp.bfloat16)

    def tile(n, step):
        tile_at = pl.ds(pl.multiple_of(((place_ref[3] >> 1) ^ step) * QT, QT), QT)
        for head in range(heads):
            columns = slice(head * DH, (head + 1) * DH)
            scores = scores_of(scaled_query(q_ref[tile_at, columns]), keys[...])
            top = jnp.max(scores, axis=1, keepdims=True)
            weights = jnp.exp2(scores - top).astype(jnp.bfloat16)
            sums = jnp.dot(weights, values[...], preferred_element_type=jnp.float32)
            total = sums[:, DH:]
            held[n, :, columns] = sums[:, :DH] / total
            held[n, :, wide + head : wide + head + 1] = (top + jnp.log2(total))[:, :1]
        pltpu.make_async_copy(held.at[n], own_ref.at[n], sent.at[n]).start()

    for n, step in enumerate(steps):
        tile(n, step)
    for n in range(len(steps)):
        pltpu.make_async_copy(held.at[n], own_ref.at[n], sent.at[n]).wait()


def far_kernel(heads, steps, slots, ids_ref, place_ref, q_ref, *rest):
    outs = len(steps) * 2
    own_ref, rest = rest[0], rest[1:]
    pieces, out_refs, (far, held, ready, here) = rest[: -4 - outs], rest[-4 - outs : -4], rest[-4:]
    wide = heads * DH
    for n, step in enumerate(steps):
        pltpu.make_async_copy(own_ref.at[step], held.at[n], here.at[n]).start()
    half_blocks = pieces[0].shape[0] // 2
    bits = half_blocks.bit_length() - 1
    plane, core, part, place = [place_ref[n] for n in range(4)]
    tiles = [(place >> 1) ^ step for step in steps]

    def fetch(source, block, n, j):
        to = pl.ds(pl.multiple_of(j * BK, BK), BK)
        pltpu.make_async_copy(
            source.at[block], far.at[n, to, pl.ds(DH, 2 * DH)], ready.at[n]
        ).start()

    def fetch_from(low, high, at, block, n, j):
        if high - low == 1:
            fetch(pieces[low], block, n, j)
            return
        middle = (low + high) // 2
        lax.cond(
            at < middle,
            lambda: fetch_from(low, middle, at, block, n, j),
            lambda: fetch_from(middle, high, at, block, n, j),
        )

    for n, tile in enumerate(tiles):

        def slot(j, carry):
            listed = ids_ref[tile * slots + j]
            number = jnp.maximum(listed, 0)
            span, half = number >> (bits + 1), (number >> bits) & 1
            back = plane - (span >> 1)
            sibling, other = (span & 1) ^ core, half ^ part
            block = (number & (half_blocks - 1)) ^ (half * (half_blocks // 2))
            apart = back == 2
            at = back * 2 + sibling + jnp.where(apart, sibling + other, 0) + 2 * (back >> 1) * (back & 1)
            block = jnp.where(apart, block, block + other * half_blocks)
            at, block = jnp.where(listed >= 0, at, 0), jnp.where(listed >= 0, block, 0)
            fetch_from(0, len(pieces), at, block, n, j)
            return carry

        lax.fori_loop(0, slots, slot, 0)

    for n, tile in enumerate(tiles):
        landed = far.at[n, :, pl.ds(DH, 2 * DH)]
        pltpu.make_async_copy(landed, landed, ready.at[n]).wait()
        far[n, :, :DH] = far[n, :, DH : 2 * DH]
        far[n, :, 3 * DH :] = jnp.ones((slots * BK, DH), jnp.bfloat16)
        for j in range(slots):

            @pl.when(ids_ref[tile * slots + j] < 0)
            def _():
                far[n, j * BK : (j + 1) * BK, 2 * DH :] = jnp.zeros((BK, 2 * DH), jnp.bfloat16)

        at = pl.ds(pl.multiple_of(tile * QT, QT), QT)
        pltpu.make_async_copy(own_ref.at[0], held.at[n], here.at[n]).wait()
        columns = [slice(head * DH, (head + 1) * DH) for head in range(heads)]
        keys, values = far[n, :, : 2 * DH], far[n, :, 2 * DH :]
        scores = [scores_of(scaled_query(q_ref[at, column]), keys) for column in columns]
        own_size = [held[n, :, wide + head : wide + head + 1] for head in range(heads)]
        tops = [
            jnp.maximum(jnp.max(score, axis=1, keepdims=True), size)
            for score, size in zip(scores, own_size)
        ]
        weights = [jnp.exp2(score - top).astype(jnp.bfloat16) for score, top in zip(scores, tops)]
        sums = [jnp.dot(w, values, preferred_element_type=jnp.float32) for w in weights]
        for head, column in enumerate(columns):
            share = jnp.exp2(own_size[head] - tops[head])
            total = share + sums[head][:, DH:]
            result = (held[n, :, column] * share + sums[head][:, :DH]) / total
            upper, lower = result[: QT // 2], result[QT // 2 :]
            odd = (place & 1) == 1
            out_refs[2 * n][:, column] = jnp.where(odd, lower, upper).astype(jnp.bfloat16)
            out_refs[2 * n + 1][:, column] = jnp.where(odd, upper, lower).astype(jnp.bfloat16)


def unpack_kernel(place_ref, *refs):
    width = refs[0].shape[1]
    for step, ref in enumerate(refs[:-1]):
        at = pl.multiple_of((place_ref[3] ^ step) * width, width)
        refs[-1][0, :, pl.ds(at, width)] = ref[...]


def pack(key_states, value_states):
    rows, heads = key_states.shape[1], key_states.shape[2] // DH
    whole = pl.BlockSpec(memory_space=pltpu.VMEM)
    return pl.pallas_call(
        pack_kernel,
        out_shape=jax.ShapeDtypeStruct((heads, rows, 2 * DH), key_states.dtype),
        in_specs=[whole] * 2,
        out_specs=whole,
        name="pack",
    )(key_states, value_states)


def unpack(place, parts):
    rows, width = parts[0].shape
    whole = pl.BlockSpec(memory_space=pltpu.VMEM)
    return pl.pallas_call(
        unpack_kernel,
        out_shape=jax.ShapeDtypeStruct((1, rows, width * len(parts)), parts[0].dtype),
        in_specs=[pl.BlockSpec(memory_space=pltpu.SMEM)] + [whole] * len(parts),
        out_specs=whole,
        name="unpack",
    )(place, *parts)


def own_attention(place, q, kv, steps, after):
    tiles = len(steps)
    tokens, width = tiles * QT, q.shape[1]
    heads = width // DH
    keys = kv.shape[0] * BK
    whole = pl.BlockSpec(memory_space=pltpu.VMEM)
    scores = tokens * heads * keys
    return pl.pallas_call(
        functools.partial(own_kernel, heads, steps),
        out_shape=jax.ShapeDtypeStruct((OWN_SLOTS, QT, width + DH), jnp.float32),
        in_specs=[pl.BlockSpec(memory_space=pltpu.SMEM)]
        + [whole] * 2
        + [pl.BlockSpec(memory_space=pl.ANY)] * len(after),
        out_specs=pl.BlockSpec(memory_space=pl.ANY),
        scratch_shapes=[pltpu.VMEM((keys, 2 * DH), jnp.bfloat16)] * 2
        + [pltpu.VMEM((tiles, QT, width + DH), jnp.float32), pltpu.SemaphoreType.DMA((tiles,))],
        cost_estimate=pl.CostEstimate(
            flops=8 * scores * DH, bytes_accessed=8 * tokens * width, transcendentals=scores
        ),
        compiler_params=pltpu.CompilerParams(vmem_limit_bytes=OWN_VMEM),
        name="own_attention",
    )(place, q, kv, *after)


def far_attention(ids, place, q, own, pieces, steps, slots):
    width = q.shape[1]
    heads = width // DH
    whole = pl.BlockSpec(memory_space=pltpu.VMEM)
    scalars = pl.BlockSpec(memory_space=pltpu.SMEM)
    anywhere = pl.BlockSpec(memory_space=pl.ANY)
    scores = len(steps) * QT * heads * slots * BK
    return pl.pallas_call(
        functools.partial(far_kernel, heads, steps, slots),
        out_shape=[jax.ShapeDtypeStruct((QT // 2, width), jnp.bfloat16)] * (2 * len(steps)),
        in_specs=[scalars] * 2
        + [whole]
        + [anywhere] * (1 + len(pieces)),
        out_specs=[whole] * (2 * len(steps)),
        scratch_shapes=[
            pltpu.VMEM((len(steps), slots * BK, 4 * DH), jnp.bfloat16),
            pltpu.VMEM((len(steps), QT, width + DH), jnp.float32),
            pltpu.SemaphoreType.DMA((len(steps),)),
            pltpu.SemaphoreType.DMA((len(steps),)),
        ],
        cost_estimate=pl.CostEstimate(
            flops=8 * scores * DH, bytes_accessed=8 * q.size, transcendentals=scores
        ),
        compiler_params=pltpu.CompilerParams(vmem_limit_bytes=FAR_VMEM),
        name="far_attention",
    )(ids, place, q, own, *pieces)


def on_device(queries, key_states, value_states, block_lists):
    tok_rows = queries.shape[1]
    model_width = queries.shape[2]
    kv_heads = key_states.shape[2] // DH
    spans = lax.axis_size("span")
    width = model_width // kv_heads
    place = lax.axis_index("seq")
    part = place // kv_heads
    turned = kv_heads // 2
    group = (place % kv_heads) ^ (part * turned)
    span = lax.axis_index("span")
    tile_count, slots = block_lists.shape[2], block_lists.shape[3]
    tiles = tile_count // 2
    rings = [[c * kv_heads + (j ^ (c * turned)) for j in range(kv_heads)] for c in range(2)]

    def turn(x):
        return lax.ppermute(x, "seq", [pair for a, b in zip(*rings) for pair in ((a, b), (b, a))])

    def trade(x, step):
        pairs = [(ring[j], ring[j ^ step]) for ring in rings for j in range(kv_heads)]
        return lax.ppermute(x, "seq", pairs)

    def shift(x, by):
        return lax.ppermute(x, "span", [(i, (i + by) % spans) for i in range(spans)])

    def swap(x):
        return lax.ppermute(x, "span", [(i, i ^ 1) for i in range(spans)])

    where = jnp.stack([span // 2, span % 2, part, group]).astype(jnp.int32)
    sent = pack(key_states, value_states)
    near = lax.all_to_all(sent, "seq", 0, 0, tiled=True, axis_index_groups=rings)
    q_send = jnp.transpose(queries[0].reshape(tok_rows, kv_heads, width), (1, 0, 2))
    q = lax.all_to_all(q_send, "seq", 0, 0, tiled=True, axis_index_groups=rings)
    q = q.reshape(kv_heads * tok_rows, width)

    other = turn(near)
    two_near = shift(near, 4)
    kv = jnp.concatenate([near, other], axis=0)
    up, down = shift(kv, 2), shift(kv, -2)
    two_other = turn(two_near)
    swap_kv, swap_two = swap(kv), swap(two_near)
    own = own_attention(where, q, kv, range(tiles), [])
    own, up, down, two_other = lax.optimization_barrier((own, up, down, two_other))
    pieces = [kv, swap_kv, up, swap(up), two_near, two_other, swap_two, swap(two_other)]
    pieces += [down, swap(down)]
    ids = lax.dynamic_slice(block_lists, (0, group, part * tiles, 0), (1, 1, tiles, slots))[0, 0]
    ids = jnp.where(part == 0, ids, jnp.roll(ids, tiles // 2, axis=0))
    ids = ids.reshape(tiles * slots)
    parts = [None] * kv_heads
    for steps in ((2, 3, 1), (0,)):
        results = far_attention(ids, where, q, own, pieces, steps, slots)
        for n, step in enumerate(steps):
            parts[2 * step] = results[2 * n]
            parts[2 * step + 1] = results[2 * n + 1]
        for step in [s for t in steps for s in (2 * t, 2 * t + 1) if s]:
            parts[step] = trade(parts[step], step)
    return unpack(where, parts)


def solution(mesh):
    in_specs = (
        P("span", "seq", None),
        P("span", "seq", None),
        P("span", "seq", None),
        P("span", None, None, None),
    )
    out_specs = P("span", "seq", None)
    return jax.shard_map(
        on_device, mesh=mesh, in_specs=in_specs, out_specs=out_specs, check_vma=False
    )
```
